512 devices in a mesh: diag: 32 (over y, z_lo), col: 16 (over z_hi, x, core).
Axes of the slice: x: 4, y: 8, z: 8 (z_hi: 2, z_lo: 4; z = z_hi * 4 + z_lo), core: 2. Of those that a mesh axis runs over, the one named last changes fastest.
Arguments:
- block_vectors: bfloat16 [8, 262144], P(None, ('diag', 'col')), may hold values from -6 to 6
- tile_blocks: bfloat16 [32, 16, 64, 128, 128], P('diag', 'col'), may hold values from -0.09375 to 0.09375
- tile_rows: int32 [32, 16, 64], P('diag', 'col'), may hold values from 0 to 63
- tile_cols: int32 [32, 16, 64], P('diag', 'col'), may hold values from 0 to 63
Outputs:
- applied: float32 [8, 262144], P(None, ('diag', 'col'))
The draws below stay inside these ranges and needn't reach their ends.
All inputs are finite; a program needn't handle non-finite values.
Results may differ from the reference program's by a relative error of at most 0.0003.
Values may be sent and summed in bfloat16 or wider, within the bound.
A program may use at most 64 MiB of HBM per device.

```python
import jax
import jax.numpy as jnp
from jax import lax

VECS = 8
TILE = 128
SEG = 512
TILES_DEV = 64
ROWS = 262144
N_DIAG = 32
N_COL = 16


def touch_ends(array, own_key, smallest, top_value):
    index_at = [jax.random.randint(jax.random.fold_in(own_key, axis), (), 0, length) for axis, length in enumerate(array.shape)]
    main_axis = array.shape.index(max(array.shape))
    next_to = index_at[:main_axis] + [(index_at[main_axis] + 1) % array.shape[main_axis]] + index_at[main_axis + 1:]
    return array.at[tuple(index_at)].set(smallest).at[tuple(next_to)].set(top_value)


def block_scale(stream_key, shape, cuts, smallest, high):
    factor_of, own = 1.0, jax.random.fold_in(stream_key, 6)
    for position, blocks in cuts:
        heights = jnp.exp(jax.random.uniform(jax.random.fold_in(own, position), (blocks,), jnp.float32, smallest / len(cuts), high / len(cuts)))
        factor_of = factor_of * jnp.repeat(heights, shape[position] // blocks).reshape([-1 if axis == position else 1 for axis in range(len(shape))])
    return factor_of


def noise(stream_key, dims, scale, limit, split=(), held_as=jnp.bfloat16):
    result = jax.random.normal(stream_key, dims, jnp.float32) * scale
    if len(split) > 0:
        result = block_scale(stream_key, dims, split, -0.22, 0.18) * result
    return jnp.clip(result, min=-limit, max=limit).astype(held_as)


def setup_inputs(seed: int = 0) -> dict:
    splits = jax.random.split(jax.random.key(seed), 5)
    return {
        "block_vectors": noise(splits[0], (VECS, ROWS), 1.0, 6.0, ((1, 512),)),
        "tile_blocks": noise(splits[1], (N_DIAG, N_COL, TILES_DEV, TILE, TILE), (2 * TILES_DEV * TILE * TILE // SEG) ** -0.5, 0.09375, ((0, 32), (1, 16))),
        "tile_rows": touch_ends(jax.random.randint(splits[2], (N_DIAG, N_COL, TILES_DEV), 0, SEG * N_COL // TILE), jax.random.fold_in(splits[2], 1), 0, (SEG * N_COL // TILE) - 1).astype(jnp.int32),
        "tile_cols": touch_ends(jax.random.randint(splits[3], (N_DIAG, N_COL, TILES_DEV), 0, SEG * N_COL // TILE), jax.random.fold_in(splits[3], 1), 0, (SEG * N_COL // TILE) - 1).astype(jnp.int32),
    }


def reference(block_vectors, tile_blocks, tile_rows, tile_cols):
    vectors = block_vectors.shape[0]
    group_blocks = SEG * N_COL // TILE
    all_blocks = group_blocks * N_DIAG
    blocked = block_vectors.reshape(vectors, all_blocks, TILE)

    def accumulate(total, diag_pos):
        dense = lax.dynamic_index_in_dim(tile_blocks, diag_pos, 0, keepdims=False).astype(jnp.float32)
        rows_here = lax.dynamic_index_in_dim(tile_rows, diag_pos, 0, keepdims=False)
        cols_here = lax.dynamic_index_in_dim(tile_cols, diag_pos, 0, keepdims=False)
        offsets = ((diag_pos - jnp.arange(N_COL, dtype=jnp.int32)) % N_DIAG).astype(jnp.int32)
        row_global = (diag_pos * group_blocks + rows_here).astype(jnp.int32)
        col_global = (offsets[:, None] * group_blocks + cols_here).astype(jnp.int32)
        far_input = blocked[:, col_global].astype(jnp.float32)
        near_input = blocked[:, row_global].astype(jnp.float32)
        row_terms = jnp.einsum('ctij,vctj->vcti', dense, far_input)
        col_terms = jnp.einsum('ctij,vcti->vctj', dense, near_input)
        total = total.at[:, row_global].add(row_terms)
        total = total.at[:, col_global].add(col_terms)
        return total, None

    start = jnp.zeros((vectors, all_blocks, TILE), jnp.float32)
    total, _ = lax.scan(accumulate, start, jnp.arange(N_DIAG, dtype=jnp.int32))
    return total.reshape(vectors, all_blocks * TILE)
```

```python
import functools

import jax
import jax.numpy as jnp
from jax import lax
from jax.experimental import pallas as pl
from jax.experimental.pallas import tpu as pltpu
from jax.sharding import PartitionSpec as P

MESH = pl.DeviceIdType.MESH
TILE = 128
VECS = 8


def kernel(
    groups, cols, tiles_n, group_blocks,
    x_ref, rows_s, cols_s, rows_v, cols_v, tiles_hbm, out_ref,
    tiles, xall, xf, terms, prow, pcol, rbuf,
    tile_sem, near_sem, far_sem, row_sem, col_sem, insend_sem, outsend_sem,
):
    seg_blocks = group_blocks // cols
    seg = seg_blocks * VECS
    whole = group_blocks * VECS
    d = lax.axis_index("diag")
    c = lax.axis_index("col")
    far_d = lax.rem(d - c + groups, groups)

    load = pltpu.make_async_copy(tiles_hbm.at[0, 0], tiles, tile_sem)
    load.start()

    barrier = pltpu.get_barrier_semaphore()

    with jax.named_scope("greet"):
        def greet_group(k, _):
            pl.semaphore_signal(barrier, inc=1, device_id=(d, lax.rem(c + k, cols)), device_id_type=MESH)
            return 0

        def greet_far(k, _):
            pl.semaphore_signal(barrier, inc=1, device_id=(far_d, k), device_id_type=MESH)
            return 0

        lax.fori_loop(1, cols, greet_group, 0)

        @pl.when(c != 0)
        def _():
            lax.fori_loop(0, cols, greet_far, 0)

        x = x_ref[...]
        own = jnp.concatenate([x[:, b * TILE:(b + 1) * TILE] for b in range(seg_blocks)], axis=0)
        xall[pl.ds(pl.multiple_of(c * seg, seg), seg), :] = own

        pl.semaphore_wait(barrier, 2 * (cols - 1))

    def own_slot(half):
        return xall.at[pl.ds(pl.multiple_of(half * whole + c * seg, seg), seg)]

    with jax.named_scope("send_input"):
        def send_far(k, _):
            pltpu.make_async_remote_copy(
                src_ref=own_slot(0), dst_ref=own_slot(1), send_sem=insend_sem, recv_sem=far_sem,
                device_id=(lax.rem(d + k, groups), k), device_id_type=MESH,
            ).start()
            return 0

        def send_near(k, _):
            pltpu.make_async_remote_copy(
                src_ref=own_slot(0), dst_ref=own_slot(0), send_sem=insend_sem, recv_sem=near_sem,
                device_id=(d, lax.rem(c + k, cols)), device_id_type=MESH,
            ).start()
            return 0

        lax.fori_loop(1, cols, send_near, 0)
        lax.fori_loop(1, cols, send_far, 0)

    g_id = lax.broadcasted_iota(jnp.int32, (group_blocks, 2 * tiles_n), 0)
    block_of = lax.rem(g_id, cols) * seg_blocks + g_id // cols

    def onehot(ids_ref):
        ids = ids_ref[0]
        ids = jnp.concatenate([ids, ids], axis=1)
        return jnp.where(block_of == ids, 1.0, 0.0).astype(jnp.bfloat16)

    def scatter(ids_ref, part):
        place = onehot(ids_ref)
        for v in range(VECS):
            t = terms[pl.ds(v, tiles_n, stride=VECS), :]
            hi = t.astype(jnp.bfloat16)
            lo = (t - hi.astype(jnp.float32)).astype(jnp.bfloat16)
            both = jnp.concatenate([hi, lo], axis=0)
            r = jnp.dot(place, both, preferred_element_type=jnp.float32)
            for b in range(seg_blocks):
                part[pl.ds(b * VECS + v, cols, stride=seg), :] = r[b * cols:(b + 1) * cols, :]

    unroll = 8

    def wait_bytes(ref, sem):
        pltpu.make_async_copy(ref, ref, sem).wait()

    with jax.named_scope("wait_tiles"):
        load.wait()
    with jax.named_scope("wait_near"):
        wait_bytes(xall.at[pl.ds(0, (cols - 1) * seg)], near_sem)

    with jax.named_scope("column_terms"):
        xf[...] = xall[pl.ds(0, whole), :].astype(jnp.float32).reshape(group_blocks, VECS, TILE)

        def col_step(q, _):
            for u in range(unroll):
                t = q * unroll + u
                near = xf[rows_s[0, 0, t]].astype(jnp.bfloat16)
                got = jnp.dot(near, tiles[t], preferred_element_type=jnp.float32)
                terms[pl.ds(pl.multiple_of(t * VECS, VECS), VECS), :] = got
            return 0

        lax.fori_loop(0, tiles_n // unroll, col_step, 0)
    with jax.named_scope("column_scatter"):
        scatter(cols_v, pcol)

    def seg_of(ref, s):
        return ref.at[pl.ds(pl.multiple_of(s * seg, seg), seg)]

    with jax.named_scope("wait_far"):
        @pl.when(c != 0)
        def _():
            wait_bytes(xall.at[pl.ds(whole, whole)], far_sem)

    with jax.named_scope("send_column"):
        def send_col(k, _):
            pltpu.make_async_remote_copy(
                src_ref=seg_of(pcol, k), dst_ref=seg_of(rbuf, cols + c),
                send_sem=outsend_sem, recv_sem=col_sem,
                device_id=(far_d, k), device_id_type=MESH,
            ).start()
            return 0

        @pl.when(c != 0)
        def _():
            lax.fori_loop(0, cols, send_col, 0)

    with jax.named_scope("row_terms"):
        base = whole * ((c + cols - 1) // cols)
        far_x = xall[pl.ds(pl.multiple_of(base, whole), whole), :].astype(jnp.float32)
        xf[...] = far_x.reshape(group_blocks, VECS, TILE)

        def row_step(q, _):
            for u in range(unroll):
                t = q * unroll + u
                far = xf[cols_s[0, 0, t]].astype(jnp.bfloat16)
                got = lax.dot_general(
                    far, tiles[t], (((1,), (1,)), ((), ())), preferred_element_type=jnp.float32
                )
                terms[pl.ds(pl.multiple_of(t * VECS, VECS), VECS), :] = got
            return 0

        lax.fori_loop(0, tiles_n // unroll, row_step, 0)
    with jax.named_scope("row_scatter"):
        scatter(rows_v, prow)

        @pl.when(c == 0)
        def _():
            prow[...] += pcol[...]

    with jax.named_scope("send_row"):
        def send_row(k, _):
            to = lax.rem(c + k, cols)
            pltpu.make_async_remote_copy(
                src_ref=seg_of(prow, to), dst_ref=seg_of(rbuf, c),
                send_sem=outsend_sem, recv_sem=row_sem,
                device_id=(d, to), device_id_type=MESH,
            ).start()
            return 0

        lax.fori_loop(1, cols, send_row, 0)

    with jax.named_scope("wait_column"):
        wait_bytes(rbuf.at[pl.ds(0, (cols - 1) * seg)], col_sem)
    with jax.named_scope("wait_row"):
        wait_bytes(rbuf.at[pl.ds(0, (cols - 1) * seg)], row_sem)

    with jax.named_scope("total"):
        total = prow[pl.ds(pl.multiple_of(c * seg, seg), seg), :]
        for k in range(1, cols):
            total += rbuf[pl.ds((cols + k) * seg, seg), :]
            total += rbuf[pl.ds(pl.multiple_of(lax.rem(c + k, cols) * seg, seg), seg), :]
        for b in range(seg_blocks):
            out_ref[:, b * TILE:(b + 1) * TILE] = total[b * VECS:(b + 1) * VECS, :]

    with jax.named_scope("wait_sent"):
        wait_bytes(xall.at[pl.ds(0, 2 * (cols - 1) * seg)], insend_sem)
        wait_bytes(prow.at[pl.ds(0, (cols - 1) * seg)], outsend_sem)

        @pl.when(c != 0)
        def _():
            wait_bytes(pcol, outsend_sem)


def body(block_vectors, tile_blocks, tile_rows, tile_cols):
    vectors, segment = block_vectors.shape
    groups = lax.axis_size("diag")
    cols = lax.axis_size("col")
    tiles_n = tile_blocks.shape[2]
    group_blocks = segment * cols // TILE
    whole = group_blocks * vectors
    vmem = pl.BlockSpec(memory_space=pltpu.VMEM)
    smem = pl.BlockSpec(memory_space=pltpu.SMEM)
    dma = pltpu.SemaphoreType.DMA
    return pl.pallas_call(
        functools.partial(kernel, groups, cols, tiles_n, group_blocks),
        out_shape=jax.ShapeDtypeStruct((vectors, segment), jnp.float32),
        in_specs=[vmem, smem, smem, vmem, vmem, pl.BlockSpec(memory_space=pl.ANY)],
        out_specs=vmem,
        scratch_shapes=[
            pltpu.VMEM((tiles_n, TILE, TILE), jnp.bfloat16),
            pltpu.VMEM((2 * whole, TILE), jnp.bfloat16),
            pltpu.VMEM((group_blocks, vectors, TILE), jnp.float32),
            pltpu.VMEM((tiles_n * vectors, TILE), jnp.float32),
            pltpu.VMEM((whole, TILE), jnp.float32),
            pltpu.VMEM((whole, TILE), jnp.float32),
            pltpu.VMEM((2 * whole, TILE), jnp.float32),
            dma, dma, dma, dma, dma, dma, dma,
        ],
        compiler_params=pltpu.CompilerParams(
            collective_id=0, has_side_effects=True, vmem_limit_bytes=32 * 1024 * 1024
        ),
    )(block_vectors, tile_rows, tile_cols, tile_rows, tile_cols, tile_blocks)


def solution(mesh):
    return jax.shard_map(
        body,
        mesh=mesh,
        in_specs=(
            P(None, ("diag", "col")),
            P("diag", "col", None, None, None),
            P("diag", "col", None),
            P("diag", "col", None),
        ),
        out_specs=P(None, ("diag", "col")),
        check_vma=False,
    )
```

```python
import functools

import jax
import jax.numpy as jnp
from jax import lax
from jax.experimental import pallas as pl
from jax.experimental.pallas import tpu as pltpu
from jax.sharding import PartitionSpec as P

MESH = pl.DeviceIdType.MESH
TILE = 128
VECS = 8
STEPS = 64.0
FULL = 32700.0
SMALLEST = 2.0 ** -110


def kernel(
    groups, cols, tiles_n, group_blocks,
    x_hbm, rows_hbm, cols_hbm, tiles_hbm, out_ref,
    x_own, rows_s, cols_s, rows_v, cols_v, tiles, flipped, xall, xf, terms, prow, pcol,
    row_words, col_words, got,
    x_sem, ids_sem, tile_sem, near_sem, far_sem, row_sem, col_sem, insend_sem, outsend_sem,
):
    seg_blocks = group_blocks // cols
    seg = seg_blocks * VECS
    half = seg // 2
    whole = group_blocks * VECS
    half_cols = cols // 2
    d = lax.axis_index("diag")
    c = lax.axis_index("col")
    far_d = lax.rem(d - c + groups, groups)

    x_load = pltpu.make_async_copy(x_hbm, x_own, x_sem)
    x_load.start()
    id_loads = [
        pltpu.make_async_copy(src.at[0], dst, ids_sem.at[n])
        for n, (src, dst) in enumerate(
            ((rows_hbm, rows_s), (cols_hbm, cols_s), (rows_hbm, rows_v), (cols_hbm, cols_v))
        )
    ]
    for load in id_loads:
        load.start()
    tile_load = pltpu.make_async_copy(tiles_hbm.at[0, 0], tiles, tile_sem)
    tile_load.start()

    def peer(j):
        this_half = c // half_cols
        other = (1 - this_half) * half_cols + lax.rem(c + j, half_cols)
        same = this_half * half_cols + lax.rem(c + j + 1, half_cols)
        crosses = 1 - j // half_cols
        return crosses * other + (1 - crosses) * same

    barrier = pltpu.get_barrier_semaphore()

    def greet_group(j, _):
        pl.semaphore_signal(barrier, inc=1, device_id=(d, peer(j)), device_id_type=MESH)
        return 0

    def greet_far(k, _):
        pl.semaphore_signal(barrier, inc=1, device_id=(far_d, k), device_id_type=MESH)
        return 0

    @pl.when(c != 0)
    def _():
        lax.fori_loop(0, cols, greet_far, 0)

    lax.fori_loop(0, cols - 1, greet_group, 0)

    x_load.wait()
    x = x_own[...]
    own = jnp.concatenate([x[:, b * TILE:(b + 1) * TILE] for b in range(seg_blocks)], axis=0)
    xall[pl.ds(pl.multiple_of(c * seg, seg), seg), :] = own

    pl.semaphore_wait(barrier, 2 * (cols - 1))

    def own_slot(side):
        return xall.at[pl.ds(pl.multiple_of(side * whole + c * seg, seg), seg)]

    def send_far(j, _):
        k = cols - 1 - j
        pltpu.make_async_remote_copy(
            src_ref=own_slot(0), dst_ref=own_slot(1), send_sem=insend_sem, recv_sem=far_sem,
            device_id=(lax.rem(d + k, groups), k), device_id_type=MESH,
        ).start()
        return 0

    def send_near(j, _):
        pltpu.make_async_remote_copy(
            src_ref=own_slot(0), dst_ref=own_slot(0), send_sem=insend_sem, recv_sem=near_sem,
            device_id=(d, peer(j)), device_id_type=MESH,
        ).start()
        return 0

    lax.fori_loop(0, cols - 1, send_near, 0)
    lax.fori_loop(0, cols - 1, send_far, 0)

    for load in id_loads:
        load.wait()
    tile_load.wait()

    def flip(q, _):
        for u in range(8):
            flipped[q * 8 + u] = tiles[q * 8 + u].T
        return 0

    lax.fori_loop(0, tiles_n // 8, flip, 0)

    g_id = lax.broadcasted_iota(jnp.int32, (group_blocks, 2 * tiles_n), 0)
    block_of = lax.rem(g_id, cols) * seg_blocks + g_id // cols

    def apply(ids_s, matrices):
        for t in range(tiles_n):
            picked = xf[ids_s[0, t]].astype(jnp.bfloat16)
            terms[t * VECS:(t + 1) * VECS, :] = jnp.dot(
                picked, matrices[t], preferred_element_type=jnp.float32
            )

    def scatter(ids_v, part):
        ids = ids_v[...]
        ids = jnp.concatenate([ids, ids], axis=1)
        place = jnp.where(block_of == ids, 1.0, 0.0).astype(jnp.bfloat16)
        for v in range(VECS):
            t = terms[pl.ds(v, tiles_n, stride=VECS), :]
            hi = t.astype(jnp.bfloat16)
            lo = (t - hi.astype(jnp.float32)).astype(jnp.bfloat16)
            both = jnp.concatenate([hi, lo], axis=0)
            r = jnp.dot(place, both, preferred_element_type=jnp.float32)
            for b in range(seg_blocks):
                part[pl.ds(b * VECS + v, cols, stride=seg), :] = r[b * cols:(b + 1) * cols, :]

    def encode(part, words):
        for s in range(cols):
            p = part[s * seg:(s + 1) * seg, :]
            top = jnp.max(jnp.abs(p), axis=0, keepdims=True)
            level = jnp.ceil(jnp.log2(jnp.maximum(top, SMALLEST)) * STEPS)
            scale = jnp.exp2(level * (-1.0 / STEPS)) * FULL
            q = jnp.round(p * scale).astype(jnp.int32)
            words[s, 0:half, :] = (q[:half, :] << 16) | (q[half:, :] & 0xFFFF)
            words[s, half:half + 1, :] = level.astype(jnp.int32)

    def wait_bytes(ref, sem):
        pltpu.make_async_copy(ref, ref, sem).wait()

    wait_bytes(xall.at[pl.ds(0, (cols - 1) * seg)], near_sem)
    xf[...] = xall[pl.ds(0, whole), :].astype(jnp.float32).reshape(group_blocks, VECS, TILE)
    apply(rows_s, tiles)
    scatter(cols_v, pcol)
    encode(pcol, col_words)

    @pl.when(c != 0)
    def _():
        wait_bytes(xall.at[pl.ds(whole, whole)], far_sem)

    def send_col(k, _):
        pltpu.make_async_remote_copy(
            src_ref=col_words.at[k], dst_ref=got.at[cols + c],
            send_sem=outsend_sem, recv_sem=col_sem,
            device_id=(far_d, k), device_id_type=MESH,
        ).start()
        return 0

    @pl.when(c != 0)
    def _():
        lax.fori_loop(0, cols, send_col, 0)

    base = whole * ((c + cols - 1) // cols)
    far_x = xall[pl.ds(pl.multiple_of(base, whole), whole), :].astype(jnp.float32)
    xf[...] = far_x.reshape(group_blocks, VECS, TILE)
    apply(cols_s, flipped)
    scatter(rows_v, prow)

    @pl.when(c == 0)
    def _():
        prow[...] += pcol[...]

    encode(prow, row_words)

    def send_row(j, _):
        to = peer(j)
        pltpu.make_async_remote_copy(
            src_ref=row_words.at[to], dst_ref=got.at[c],
            send_sem=outsend_sem, recv_sem=row_sem,
            device_id=(d, to), device_id_type=MESH,
        ).start()
        return 0

    lax.fori_loop(0, cols - 1, send_row, 0)

    mine = prow[pl.ds(pl.multiple_of(c * seg, seg), seg), :]
    upper, lower = mine[:half, :], mine[half:, :]

    def add(slot, upper, lower):
        w = got[slot, 0:half, :]
        unit = jnp.exp2(got[slot, half:half + 1, :].astype(jnp.float32) * (1.0 / STEPS)) * (1.0 / FULL)
        upper += (w >> 16).astype(jnp.float32) * unit
        lower += ((w << 16) >> 16).astype(jnp.float32) * unit
        return upper, lower

    wait_bytes(got.at[pl.ds(0, cols - 1)], row_sem)
    for k in range(1, cols):
        upper, lower = add(lax.rem(c + k, cols), upper, lower)
    wait_bytes(got.at[pl.ds(0, cols - 1)], col_sem)
    for k in range(1, cols):
        upper, lower = add(cols + k, upper, lower)

    total = jnp.concatenate([upper, lower], axis=0)
    for b in range(seg_blocks):
        out_ref[:, b * TILE:(b + 1) * TILE] = total[b * VECS:(b + 1) * VECS, :]

    wait_bytes(xall.at[pl.ds(0, 2 * (cols - 1) * seg)], insend_sem)
    wait_bytes(row_words.at[pl.ds(0, cols - 1)], outsend_sem)

    @pl.when(c != 0)
    def _():
        wait_bytes(col_words, outsend_sem)


def body(block_vectors, tile_blocks, tile_rows, tile_cols):
    vectors, segment = block_vectors.shape
    groups = lax.axis_size("diag")
    cols = lax.axis_size("col")
    tiles_n = tile_blocks.shape[2]
    group_blocks = segment * cols // TILE
    whole = group_blocks * vectors
    seg = whole // cols
    hbm = pl.BlockSpec(memory_space=pltpu.HBM)
    dma = pltpu.SemaphoreType.DMA
    return pl.pallas_call(
        functools.partial(kernel, groups, cols, tiles_n, group_blocks),
        out_shape=jax.ShapeDtypeStruct((vectors, segment), jnp.float32),
        in_specs=[hbm, hbm, hbm, hbm],
        out_specs=pl.BlockSpec(memory_space=pltpu.VMEM),
        scratch_shapes=[
            pltpu.VMEM((vectors, segment), jnp.bfloat16),
            pltpu.SMEM((1, tiles_n), jnp.int32),
            pltpu.SMEM((1, tiles_n), jnp.int32),
            pltpu.VMEM((1, tiles_n), jnp.int32),
            pltpu.VMEM((1, tiles_n), jnp.int32),
            pltpu.VMEM((tiles_n, TILE, TILE), jnp.bfloat16),
            pltpu.VMEM((tiles_n, TILE, TILE), jnp.bfloat16),
            pltpu.VMEM((2 * whole, TILE), jnp.bfloat16),
            pltpu.VMEM((group_blocks, vectors, TILE), jnp.float32),
            pltpu.VMEM((tiles_n * vectors, TILE), jnp.float32),
            pltpu.VMEM((whole, TILE), jnp.float32),
            pltpu.VMEM((whole, TILE), jnp.float32),
            pltpu.VMEM((cols, seg // 2 + 1, TILE), jnp.int32),
            pltpu.VMEM((cols, seg // 2 + 1, TILE), jnp.int32),
            pltpu.VMEM((2 * cols, seg // 2 + 1, TILE), jnp.int32),
            dma, dma((4,)), dma, dma, dma, dma, dma, dma, dma,
        ],
        compiler_params=pltpu.CompilerParams(
            collective_id=0, has_side_effects=True, vmem_limit_bytes=32 * 1024 * 1024
        ),
    )(block_vectors, tile_rows, tile_cols, tile_blocks)


def solution(mesh):
    return jax.shard_map(
        body,
        mesh=mesh,
        in_specs=(
            P(None, ("diag", "col")),
            P("diag", "col", None, None, None),
            P("diag", "col", None),
            P("diag", "col", None),
        ),
        out_specs=P(None, ("diag", "col")),
        check_vma=False,
    )
```

```python
import functools

import jax
import jax.numpy as jnp
from jax import lax
from jax.experimental import pallas as pl
from jax.experimental.pallas import tpu as pltpu
from jax.sharding import PartitionSpec as P

MESH = pl.DeviceIdType.MESH
TILE = 128
VECS = 8
STEPS = 64.0
FULL = 32700.0
SMALLEST = 2.0 ** -110
COL_FIRST = 8


def kernel(
    groups, cols, tiles_n, group_blocks,
    x_hbm, rows_hbm, cols_hbm, tiles_hbm, out_ref,
    x_own, rows_s, cols_s, rows_v, cols_v, tiles, flipped, xall, xf, terms, prow, pcol, pair,
    row_words, col_words, got,
    x_sem, ids_sem, tile_sem, near_sem, sib_sem, far_sem, pair_sem, pair_sent_sem, row_sem, col_sem,
    insend_sem, outsend_sem,
):
    seg_blocks = group_blocks // cols
    seg = seg_blocks * VECS
    half = seg // 2
    whole = group_blocks * VECS
    d = lax.axis_index("diag")
    c = lax.axis_index("col")
    far_d = lax.rem(d - c + groups, groups)

    x_load = pltpu.make_async_copy(x_hbm, x_own, x_sem)
    x_load.start()
    id_loads = [
        pltpu.make_async_copy(src.at[0], dst, ids_sem.at[n])
        for n, (src, dst) in enumerate(
            ((rows_hbm, rows_s), (cols_hbm, cols_s), (rows_hbm, rows_v), (cols_hbm, cols_v))
        )
    ]
    for load in id_loads:
        load.start()
    tile_load = pltpu.make_async_copy(tiles_hbm.at[0, 0], tiles, tile_sem)
    tile_load.start()

    chips = cols // 2
    chip = c // 2
    core = lax.rem(c, 2)
    sibling = 2 * chip + 1 - core
    place = core * chips + chip

    def place_of(e):
        return (e % 2) * chips + e // 2

    def peer_chip(j):
        return j + (j + chips - chip) // chips

    barrier = pltpu.get_barrier_semaphore()

    def greet_group(j, _):
        pl.semaphore_signal(
            barrier, inc=1, device_id=(d, 2 * peer_chip(j) + core), device_id_type=MESH
        )
        return 0

    def greet_far(k, _):
        pl.semaphore_signal(barrier, inc=1, device_id=(far_d, k), device_id_type=MESH)
        return 0

    @pl.when(c != 0)
    def _():
        lax.fori_loop(0, cols, greet_far, 0)

    lax.fori_loop(0, chips - 1, greet_group, 0)
    pl.semaphore_signal(barrier, inc=1, device_id=(d, sibling), device_id_type=MESH)

    x_load.wait()
    x = x_own[...]
    own = jnp.concatenate([x[:, b * TILE:(b + 1) * TILE] for b in range(seg_blocks)], axis=0)
    xall[pl.ds(pl.multiple_of(place * seg, seg), seg), :] = own

    pl.semaphore_wait(barrier, chips + cols - 1)

    def own_slot(side):
        return xall.at[pl.ds(pl.multiple_of(side * whole + place * seg, seg), seg)]

    def send_far(j, _):
        k = j + 1
        pltpu.make_async_remote_copy(
            src_ref=own_slot(0), dst_ref=own_slot(1), send_sem=insend_sem, recv_sem=far_sem,
            device_id=(lax.rem(d + k, groups), k), device_id_type=MESH,
        ).start()
        return 0

    def send_near(j, _):
        pltpu.make_async_remote_copy(
            src_ref=own_slot(0), dst_ref=own_slot(0), send_sem=insend_sem, recv_sem=near_sem,
            device_id=(d, 2 * peer_chip(j) + core), device_id_type=MESH,
        ).start()
        return 0

    lax.fori_loop(0, cols - 1, send_far, 0)
    lax.fori_loop(0, chips - 1, send_near, 0)

    for load in id_loads:
        load.wait()
    tile_load.wait()

    def flip(q, _):
        for u in range(8):
            flipped[q * 8 + u] = tiles[q * 8 + u].T
        return 0

    lax.fori_loop(0, tiles_n // 8, flip, 0)

    g_id = lax.broadcasted_iota(jnp.int32, (group_blocks, 2 * tiles_n), 0)
    at = lax.rem(g_id, cols)
    col_block = at * seg_blocks + g_id // cols
    row_block = (lax.rem(at, chips) * 2 + at // chips) * seg_blocks + g_id // cols

    def apply(ids_s, matrices):
        for t in range(tiles_n):
            picked = xf[ids_s[0, t]].astype(jnp.bfloat16)
            terms[t * VECS:(t + 1) * VECS, :] = jnp.dot(
                picked, matrices[t], preferred_element_type=jnp.float32
            )

    def scatter(ids_v, block_of, part):
        ids = ids_v[...]
        ids = jnp.concatenate([ids, ids], axis=1)
        select = jnp.where(block_of == ids, 1.0, 0.0).astype(jnp.bfloat16)
        for v in range(VECS):
            t = terms[pl.ds(v, tiles_n, stride=VECS), :]
            hi = t.astype(jnp.bfloat16)
            lo = (t - hi.astype(jnp.float32)).astype(jnp.bfloat16)
            both = jnp.concatenate([hi, lo], axis=0)
            r = jnp.dot(select, both, preferred_element_type=jnp.float32)
            for b in range(seg_blocks):
                part[pl.ds(b * VECS + v, cols, stride=seg), :] = r[b * cols:(b + 1) * cols, :]

    def encode(part, first, count, words):
        for s in range(count):
            p = part[pl.ds(pl.multiple_of(first * seg, seg) + s * seg, seg), :]
            top = jnp.max(jnp.abs(p), axis=0, keepdims=True)
            level = jnp.ceil(jnp.log2(jnp.maximum(top, SMALLEST)) * STEPS)
            scale = jnp.exp2(level * (-1.0 / STEPS)) * FULL
            q = jnp.round(p * scale).astype(jnp.int32)
            words[s, 0:half, :] = (q[:half, :] << 16) | (q[half:, :] & 0xFFFF)
            words[s, half:half + 1, :] = level.astype(jnp.int32)

    def wait_bytes(ref, sem):
        pltpu.make_async_copy(ref, ref, sem).wait()

    def load_inputs(first):
        for e in range(cols):
            part = xall[pl.ds(pl.multiple_of(first, whole) + place_of(e) * seg, seg), :]
            xf[e * seg_blocks:(e + 1) * seg_blocks] = part.astype(jnp.float32).reshape(
                seg_blocks, VECS, TILE
            )

    wait_bytes(xall.at[pl.ds(0, (chips - 1) * seg)], near_sem)
    same_core = xall.at[pl.ds(pl.multiple_of(core * chips * seg, chips * seg), chips * seg)]
    pltpu.make_async_remote_copy(
        src_ref=same_core, dst_ref=same_core, send_sem=insend_sem, recv_sem=sib_sem,
        device_id=(d, sibling), device_id_type=MESH,
    ).start()
    wait_bytes(xall.at[pl.ds(0, chips * seg)], sib_sem)

    load_inputs(0)
    apply(rows_s, tiles)
    scatter(cols_v, col_block, pcol)
    encode(pcol, 0, cols, col_words)

    @pl.when(c != 0)
    def _():
        wait_bytes(xall.at[pl.ds(whole, whole)], far_sem)

    def send_col(k, _):
        pltpu.make_async_remote_copy(
            src_ref=col_words.at[k], dst_ref=got.at[chips + c],
            send_sem=outsend_sem, recv_sem=col_sem,
            device_id=(far_d, k), device_id_type=MESH,
        ).start()
        return 0

    @pl.when(c != 0)
    def _():
        lax.fori_loop(0, COL_FIRST, send_col, 0)

    load_inputs(whole * ((c + cols - 1) // cols))
    apply(cols_s, flipped)
    scatter(rows_v, row_block, prow)

    @pl.when(c == 0)
    def _():
        for e in range(cols):
            here = place_of(e) * seg
            prow[here:here + seg, :] += pcol[e * seg:(e + 1) * seg, :]

    half_rows = chips * seg
    pltpu.make_async_remote_copy(
        src_ref=prow.at[pl.ds(pl.multiple_of((1 - core) * half_rows, half_rows), half_rows)],
        dst_ref=pair, send_sem=pair_sent_sem, recv_sem=pair_sem,
        device_id=(d, sibling), device_id_type=MESH,
    ).start()
    wait_bytes(pair, pair_sem)
    ours = pl.ds(pl.multiple_of(core * half_rows, half_rows), half_rows)
    prow[ours, :] += pair[...]
    encode(prow, core * chips, chips, row_words)

    def send_row(j, _):
        to = peer_chip(j)
        pltpu.make_async_remote_copy(
            src_ref=row_words.at[to], dst_ref=got.at[chip],
            send_sem=outsend_sem, recv_sem=row_sem,
            device_id=(d, 2 * to + core), device_id_type=MESH,
        ).start()
        return 0

    lax.fori_loop(0, chips - 1, send_row, 0)

    @pl.when(c != 0)
    def _():
        lax.fori_loop(COL_FIRST, cols, send_col, 0)

    mine = prow[pl.ds(pl.multiple_of(place * seg, seg), seg), :]
    upper, lower = mine[:half, :], mine[half:, :]

    def add(slot, upper, lower):
        w = got[slot, 0:half, :]
        unit = jnp.exp2(got[slot, half:half + 1, :].astype(jnp.float32) * (1.0 / STEPS)) * (1.0 / FULL)
        upper += (w >> 16).astype(jnp.float32) * unit
        lower += ((w << 16) >> 16).astype(jnp.float32) * unit
        return upper, lower

    wait_bytes(got.at[pl.ds(0, chips - 1)], row_sem)
    for j in range(chips - 1):
        upper, lower = add(peer_chip(j), upper, lower)
    wait_bytes(got.at[pl.ds(0, cols - 1)], col_sem)
    for k in range(1, cols):
        upper, lower = add(chips + k, upper, lower)

    total = jnp.concatenate([upper, lower], axis=0)
    for b in range(seg_blocks):
        out_ref[:, b * TILE:(b + 1) * TILE] = total[b * VECS:(b + 1) * VECS, :]

    wait_bytes(xall.at[pl.ds(0, (2 * chips - 1 + cols - 1) * seg)], insend_sem)
    wait_bytes(pair, pair_sent_sem)
    wait_bytes(row_words.at[pl.ds(0, chips - 1)], outsend_sem)

    @pl.when(c != 0)
    def _():
        wait_bytes(col_words, outsend_sem)


def body(block_vectors, tile_blocks, tile_rows, tile_cols):
    vectors, segment = block_vectors.shape
    groups = lax.axis_size("diag")
    cols = lax.axis_size("col")
    tiles_n = tile_blocks.shape[2]
    group_blocks = segment * cols // TILE
    whole = group_blocks * vectors
    seg = whole // cols
    hbm = pl.BlockSpec(memory_space=pltpu.HBM)
    dma = pltpu.SemaphoreType.DMA
    return pl.pallas_call(
        functools.partial(kernel, groups, cols, tiles_n, group_blocks),
        out_shape=jax.ShapeDtypeStruct((vectors, segment), jnp.float32),
        in_specs=[hbm, hbm, hbm, hbm],
        out_specs=pl.BlockSpec(memory_space=pltpu.VMEM),
        scratch_shapes=[
            pltpu.VMEM((vectors, segment), jnp.bfloat16),
            pltpu.SMEM((1, tiles_n), jnp.int32),
            pltpu.SMEM((1, tiles_n), jnp.int32),
            pltpu.VMEM((1, tiles_n), jnp.int32),
            pltpu.VMEM((1, tiles_n), jnp.int32),
            pltpu.VMEM((tiles_n, TILE, TILE), jnp.bfloat16),
            pltpu.VMEM((tiles_n, TILE, TILE), jnp.bfloat16),
            pltpu.VMEM((2 * whole, TILE), jnp.bfloat16),
            pltpu.VMEM((group_blocks, vectors, TILE), jnp.float32),
            pltpu.VMEM((tiles_n * vectors, TILE), jnp.float32),
            pltpu.VMEM((whole, TILE), jnp.float32),
            pltpu.VMEM((whole, TILE), jnp.float32),
            pltpu.VMEM((whole // 2, TILE), jnp.float32),
            pltpu.VMEM((cols // 2, seg // 2 + 1, TILE), jnp.int32),
            pltpu.VMEM((cols, seg // 2 + 1, TILE), jnp.int32),
            pltpu.VMEM((cols // 2 + cols, seg // 2 + 1, TILE), jnp.int32),
            dma, dma((4,)), dma, dma, dma, dma, dma, dma, dma, dma, dma, dma,
        ],
        compiler_params=pltpu.CompilerParams(
            collective_id=0, has_side_effects=True, vmem_limit_bytes=32 * 1024 * 1024
        ),
    )(*[pltpu.with_memory_space_constraint(a, pltpu.HBM) for a in (block_vectors, tile_rows, tile_cols, tile_blocks)])


def solution(mesh):
    return jax.shard_map(
        body,
        mesh=mesh,
        in_specs=(
            P(None, ("diag", "col")),
            P("diag", "col", None, None, None),
            P("diag", "col", None),
            P("diag", "col", None),
        ),
        out_specs=P(None, ("diag", "col")),
        check_vma=False,
    )
```

```python
import functools

import jax
import jax.numpy as jnp
from jax import lax
from jax.experimental import pallas as pl
from jax.experimental.pallas import tpu as pltpu
from jax.sharding import PartitionSpec as P

MESH = pl.DeviceIdType.MESH
TILE = 128
VECS = 8
STEPS = 64.0
FULL = 32700.0
SMALLEST = 2.0 ** -110
COL_FIRST = 8


def kernel(
    groups, cols, tiles_n, group_blocks,
    x_hbm, rows_hbm, cols_hbm, tiles_hbm, out_ref,
    x_own, rows_s, cols_s, rows_v, cols_v, tiles, flipped, xall, xf, terms, prow, pcol, pair,
    row_words, col_words, got,
    x_sem, ids_sem, tile_sem, near_sem, sib_sem, far_sem, pair_sem, pair_sent_sem, row_sem, col_sem,
    insend_sem, outsend_sem, told,
):
    seg_blocks = group_blocks // cols
    seg = seg_blocks * VECS
    half = seg // 2
    whole = group_blocks * VECS
    d = lax.axis_index("diag")
    c = lax.axis_index("col")
    far_d = lax.rem(d - c + groups, groups)

    x_load = pltpu.make_async_copy(x_hbm, x_own, x_sem)
    x_load.start()
    id_loads = [
        pltpu.make_async_copy(src.at[0], dst, ids_sem.at[n])
        for n, (src, dst) in enumerate(
            ((rows_hbm, rows_s), (cols_hbm, cols_s), (rows_hbm, rows_v), (cols_hbm, cols_v))
        )
    ]
    for load in id_loads:
        load.start()
    tile_load = pltpu.make_async_copy(tiles_hbm.at[0, 0], tiles, tile_sem)
    tile_load.start()

    chips = cols // 2
    chip = c // 2
    core = lax.rem(c, 2)
    sibling = 2 * chip + 1 - core
    place = core * chips + chip

    def place_of(e):
        return (e % 2) * chips + e // 2

    def peer_chip(j):
        return j + (j + chips - chip) // chips

    half_chips = chips // 2
    half_cols = cols // 2
    late = chip // half_chips
    early_peers = half_chips - 1 + late
    barrier = pltpu.get_barrier_semaphore()

    def greet_far(q, _):
        pl.semaphore_signal(barrier, inc=1, device_id=(far_d, 2 * q + late), device_id_type=MESH)
        return 0

    def greet_group(j, _):
        pl.semaphore_signal(
            barrier, inc=1, device_id=(d, 2 * peer_chip(j) + late), device_id_type=MESH
        )
        return 0

    @pl.when(c != 0)
    def _():
        lax.fori_loop(0, chips, greet_far, 0)

    lax.fori_loop(0, chips - 1, greet_group, 0)
    pl.semaphore_signal(barrier, inc=1, device_id=(d, sibling), device_id_type=MESH)

    def greet_back(k, _):
        pl.semaphore_signal(
            barrier, inc=1, device_id=(lax.rem(d + k, groups), 2 * (k // 2) + late),
            device_id_type=MESH,
        )
        return 0

    lax.fori_loop(1, cols, greet_back, 0)
    back = half_cols * (1 + (chip + chips - 1) // chips)

    x_load.wait()
    x = x_own[...]
    own = jnp.concatenate([x[:, b * TILE:(b + 1) * TILE] for b in range(seg_blocks)], axis=0)
    xall[pl.ds(pl.multiple_of(place * seg, seg), seg), :] = own

    def tell_sibling():
        pl.semaphore_signal(told, inc=1, device_id=(d, sibling), device_id_type=MESH)

    @pl.when(core == 0)
    def _():
        pl.semaphore_wait(barrier, 2 * early_peers + half_cols - 1 + 1 + back)
        tell_sibling()

    @pl.when(core == 1)
    def _():
        pl.semaphore_wait(told, 1)

    def own_slot(side):
        return xall.at[pl.ds(pl.multiple_of(side * whole + place * seg, seg), seg)]

    def send_far(j, _):
        k = j + 1
        pltpu.make_async_remote_copy(
            src_ref=own_slot(0), dst_ref=own_slot(1), send_sem=insend_sem, recv_sem=far_sem,
            device_id=(lax.rem(d + k, groups), k), device_id_type=MESH,
        ).start()
        return 0

    def send_near(j, _):
        pltpu.make_async_remote_copy(
            src_ref=own_slot(0), dst_ref=own_slot(0), send_sem=insend_sem, recv_sem=near_sem,
            device_id=(d, 2 * peer_chip(j) + core), device_id_type=MESH,
        ).start()
        return 0

    lax.fori_loop(0, early_peers, send_near, 0)
    lax.fori_loop(0, half_cols - 1, send_far, 0)

    @pl.when(core == 1)
    def _():
        pl.semaphore_wait(barrier, 2 * (chips - 1 - early_peers) + half_cols + 1 + back)
        tell_sibling()

    @pl.when(core == 0)
    def _():
        pl.semaphore_wait(told, 1)

    lax.fori_loop(early_peers, chips - 1, send_near, 0)
    lax.fori_loop(half_cols - 1, cols - 1, send_far, 0)

    for load in id_loads:
        load.wait()
    tile_load.wait()

    def flip(q, _):
        for u in range(8):
            flipped[q * 8 + u] = tiles[q * 8 + u].T
        return 0

    lax.fori_loop(0, tiles_n // 8, flip, 0)

    g_id = lax.broadcasted_iota(jnp.int32, (group_blocks, 2 * tiles_n), 0)
    at = lax.rem(g_id, cols)
    col_block = at * seg_blocks + g_id // cols
    row_block = (lax.rem(at, chips) * 2 + at // chips) * seg_blocks + g_id // cols

    def apply(ids_s, matrices):
        for t in range(tiles_n):
            picked = xf[ids_s[0, t]].astype(jnp.bfloat16)
            terms[t * VECS:(t + 1) * VECS, :] = jnp.dot(
                picked, matrices[t], preferred_element_type=jnp.float32
            )

    def scatter(ids_v, block_of, part):
        ids = ids_v[...]
        ids = jnp.concatenate([ids, ids], axis=1)
        select = jnp.where(block_of == ids, 1.0, 0.0).astype(jnp.bfloat16)
        for v in range(VECS):
            t = terms[pl.ds(v, tiles_n, stride=VECS), :]
            hi = t.astype(jnp.bfloat16)
            lo = (t - hi.astype(jnp.float32)).astype(jnp.bfloat16)
            both = jnp.concatenate([hi, lo], axis=0)
            r = jnp.dot(select, both, preferred_element_type=jnp.float32)
            for b in range(seg_blocks):
                part[pl.ds(b * VECS + v, cols, stride=seg), :] = r[b * cols:(b + 1) * cols, :]

    def encode(part, first, count, words):
        for s in range(count):
            p = part[pl.ds(pl.multiple_of(first * seg, seg) + s * seg, seg), :]
            top = jnp.max(jnp.abs(p), axis=0, keepdims=True)
            level = jnp.ceil(jnp.log2(jnp.maximum(top, SMALLEST)) * STEPS)
            scale = jnp.exp2(level * (-1.0 / STEPS)) * FULL
            q = jnp.round(p * scale).astype(jnp.int32)
            words[s, 0:half, :] = (q[:half, :] << 16) | (q[half:, :] & 0xFFFF)
            words[s, half:half + 1, :] = level.astype(jnp.int32)

    def wait_bytes(ref, sem):
        pltpu.make_async_copy(ref, ref, sem).wait()

    def load_inputs(first):
        for e in range(cols):
            part = xall[pl.ds(pl.multiple_of(first, whole) + place_of(e) * seg, seg), :]
            xf[e * seg_blocks:(e + 1) * seg_blocks] = part.astype(jnp.float32).reshape(
                seg_blocks, VECS, TILE
            )

    wait_bytes(xall.at[pl.ds(0, (chips - 1) * seg)], near_sem)
    same_core = xall.at[pl.ds(pl.multiple_of(core * chips * seg, chips * seg), chips * seg)]
    pltpu.make_async_remote_copy(
        src_ref=same_core, dst_ref=same_core, send_sem=insend_sem, recv_sem=sib_sem,
        device_id=(d, sibling), device_id_type=MESH,
    ).start()
    wait_bytes(xall.at[pl.ds(0, chips * seg)], sib_sem)

    load_inputs(0)
    apply(rows_s, tiles)
    scatter(cols_v, col_block, pcol)
    encode(pcol, 0, cols, col_words)

    def send_col(k, _):
        pltpu.make_async_remote_copy(
            src_ref=col_words.at[k], dst_ref=got.at[chips + c],
            send_sem=outsend_sem, recv_sem=col_sem,
            device_id=(far_d, k), device_id_type=MESH,
        ).start()
        return 0

    @pl.when(c != 0)
    def _():
        lax.fori_loop(0, COL_FIRST, send_col, 0)

    @pl.when(c != 0)
    def _():
        wait_bytes(xall.at[pl.ds(whole, whole)], far_sem)

    load_inputs(whole * ((c + cols - 1) // cols))
    apply(cols_s, flipped)
    scatter(rows_v, row_block, prow)

    @pl.when(c == 0)
    def _():
        for e in range(cols):
            here = place_of(e) * seg
            prow[here:here + seg, :] += pcol[e * seg:(e + 1) * seg, :]

    half_rows = chips * seg
    pltpu.make_async_remote_copy(
        src_ref=prow.at[pl.ds(pl.multiple_of((1 - core) * half_rows, half_rows), half_rows)],
        dst_ref=pair, send_sem=pair_sent_sem, recv_sem=pair_sem,
        device_id=(d, sibling), device_id_type=MESH,
    ).start()
    wait_bytes(pair, pair_sem)
    ours = pl.ds(pl.multiple_of(core * half_rows, half_rows), half_rows)
    prow[ours, :] += pair[...]
    encode(prow, core * chips, chips, row_words)

    def send_row(j, _):
        to = peer_chip(j)
        pltpu.make_async_remote_copy(
            src_ref=row_words.at[to], dst_ref=got.at[chip],
            send_sem=outsend_sem, recv_sem=row_sem,
            device_id=(d, 2 * to + core), device_id_type=MESH,
        ).start()
        return 0

    lax.fori_loop(0, chips - 1, send_row, 0)

    @pl.when((late == 0) & (c != 0))
    def _():
        lax.fori_loop(COL_FIRST, cols, send_col, 0)

    mine = prow[pl.ds(pl.multiple_of(place * seg, seg), seg), :]
    upper, lower = mine[:half, :], mine[half:, :]

    def add(slot, upper, lower):
        w = got[slot, 0:half, :]
        unit = jnp.exp2(got[slot, half:half + 1, :].astype(jnp.float32) * (1.0 / STEPS)) * (1.0 / FULL)
        upper += (w >> 16).astype(jnp.float32) * unit
        lower += ((w << 16) >> 16).astype(jnp.float32) * unit
        return upper, lower

    wait_bytes(got.at[pl.ds(0, chips - 1)], row_sem)
    for j in range(chips - 1):
        upper, lower = add(peer_chip(j), upper, lower)
    @pl.when(late == 1)
    def _():
        lax.fori_loop(COL_FIRST, cols, send_col, 0)

    wait_bytes(got.at[pl.ds(0, cols - 1)], col_sem)
    for k in range(1, cols):
        upper, lower = add(chips + k, upper, lower)

    total = jnp.concatenate([upper, lower], axis=0)
    for b in range(seg_blocks):
        out_ref[:, b * TILE:(b + 1) * TILE] = total[b * VECS:(b + 1) * VECS, :]

    wait_bytes(xall.at[pl.ds(0, (2 * chips - 1 + cols - 1) * seg)], insend_sem)
    wait_bytes(pair, pair_sent_sem)
    wait_bytes(row_words.at[pl.ds(0, chips - 1)], outsend_sem)

    @pl.when(c != 0)
    def _():
        wait_bytes(col_words, outsend_sem)


def body(block_vectors, tile_blocks, tile_rows, tile_cols):
    vectors, segment = block_vectors.shape
    groups = lax.axis_size("diag")
    cols = lax.axis_size("col")
    tiles_n = tile_blocks.shape[2]
    group_blocks = segment * cols // TILE
    whole = group_blocks * vectors
    seg = whole // cols
    hbm = pl.BlockSpec(memory_space=pltpu.HBM)
    dma = pltpu.SemaphoreType.DMA
    return pl.pallas_call(
        functools.partial(kernel, groups, cols, tiles_n, group_blocks),
        out_shape=jax.ShapeDtypeStruct((vectors, segment), jnp.float32),
        in_specs=[hbm, hbm, hbm, hbm],
        out_specs=pl.BlockSpec(memory_space=pltpu.VMEM),
        scratch_shapes=[
            pltpu.VMEM((vectors, segment), jnp.bfloat16),
            pltpu.SMEM((1, tiles_n), jnp.int32),
            pltpu.SMEM((1, tiles_n), jnp.int32),
            pltpu.VMEM((1, tiles_n), jnp.int32),
            pltpu.VMEM((1, tiles_n), jnp.int32),
            pltpu.VMEM((tiles_n, TILE, TILE), jnp.bfloat16),
            pltpu.VMEM((tiles_n, TILE, TILE), jnp.bfloat16),
            pltpu.VMEM((2 * whole, TILE), jnp.bfloat16),
            pltpu.VMEM((group_blocks, vectors, TILE), jnp.float32),
            pltpu.VMEM((tiles_n * vectors, TILE), jnp.float32),
            pltpu.VMEM((whole, TILE), jnp.float32),
            pltpu.VMEM((whole, TILE), jnp.float32),
            pltpu.VMEM((whole // 2, TILE), jnp.float32),
            pltpu.VMEM((cols // 2, seg // 2 + 1, TILE), jnp.int32),
            pltpu.VMEM((cols, seg // 2 + 1, TILE), jnp.int32),
            pltpu.VMEM((cols // 2 + cols, seg // 2 + 1, TILE), jnp.int32),
            dma, dma((4,)), dma, dma, dma, dma, dma, dma, dma, dma, dma, dma,
            pltpu.SemaphoreType.REGULAR,
        ],
        compiler_params=pltpu.CompilerParams(
            collective_id=0, has_side_effects=True, vmem_limit_bytes=32 * 1024 * 1024
        ),
    )(*[pltpu.with_memory_space_constraint(a, pltpu.HBM) for a in (block_vectors, tile_rows, tile_cols, tile_blocks)])


def solution(mesh):
    return jax.shard_map(
        body,
        mesh=mesh,
        in_specs=(
            P(None, ("diag", "col")),
            P("diag", "col", None, None, None),
            P("diag", "col", None),
            P("diag", "col", None),
        ),
        out_specs=P(None, ("diag", "col")),
        check_vma=False,
    )
```

```python
import functools

import jax
import jax.numpy as jnp
from jax import lax
from jax.experimental import pallas as pl
from jax.experimental.pallas import tpu as pltpu
from jax.sharding import PartitionSpec as P

MESH = pl.DeviceIdType.MESH
TILE = 128
VECS = 8
STEPS = 64.0
FULL = 32700.0
SMALLEST = 2.0 ** -110
COL_FIRST = 8


def kernel(
    groups, cols, tiles_n, group_blocks,
    x_hbm, rows_hbm, cols_hbm, tiles_hbm, out_ref,
    x_own, rows_s, cols_s, rows_v, cols_v, tiles, flipped, xall, xf, terms, ours, theirs, pcol, pair,
    row_words, col_words, got,
    x_sem, ids_sem, tile_sem, near_sem, sib_sem, far_sem, pair_sem, pair_sent_sem, row_sem, col_sem,
    insend_sem, outsend_sem, told,
):
    seg_blocks = group_blocks // cols
    seg = seg_blocks * VECS
    half = seg // 2
    whole = group_blocks * VECS
    d = lax.axis_index("diag")
    c = lax.axis_index("col")
    far_d = lax.rem(d - c + groups, groups)

    x_load = pltpu.make_async_copy(x_hbm, x_own, x_sem)
    x_load.start()
    id_loads = [
        pltpu.make_async_copy(src.at[0], dst, ids_sem.at[n])
        for n, (src, dst) in enumerate(
            ((rows_hbm, rows_s), (cols_hbm, cols_s), (rows_hbm, rows_v), (cols_hbm, cols_v))
        )
    ]
    for load in id_loads:
        load.start()
    tile_load = pltpu.make_async_copy(tiles_hbm.at[0, 0], tiles, tile_sem)
    tile_load.start()

    chips = cols // 2
    chip = c // 2
    core = lax.rem(c, 2)
    sibling = 2 * chip + 1 - core
    place = core * chips + chip

    def place_of(e):
        return (e % 2) * chips + e // 2

    def peer_chip(j):
        return j + (j + chips - chip) // chips

    half_chips = chips // 2
    half_cols = cols // 2
    late = chip // half_chips
    early_peers = half_chips - 1 + late
    barrier = pltpu.get_barrier_semaphore()

    def greet_far(q, _):
        pl.semaphore_signal(barrier, inc=1, device_id=(far_d, 2 * q + late), device_id_type=MESH)
        return 0

    def greet_group(j, _):
        pl.semaphore_signal(
            barrier, inc=1, device_id=(d, 2 * peer_chip(j) + late), device_id_type=MESH
        )
        return 0

    @pl.when(c != 0)
    def _():
        lax.fori_loop(0, chips, greet_far, 0)

    lax.fori_loop(0, chips - 1, greet_group, 0)
    pl.semaphore_signal(barrier, inc=1, device_id=(d, sibling), device_id_type=MESH)

    def greet_back(k, _):
        pl.semaphore_signal(
            barrier, inc=1, device_id=(lax.rem(d + k, groups), 2 * (k // 2) + late),
            device_id_type=MESH,
        )
        return 0

    lax.fori_loop(1, cols, greet_back, 0)
    back = half_cols * (1 + (chip + chips - 1) // chips)

    x_load.wait()
    x = x_own[...]
    own = jnp.concatenate([x[:, b * TILE:(b + 1) * TILE] for b in range(seg_blocks)], axis=0)
    xall[pl.ds(pl.multiple_of(place * seg, seg), seg), :] = own

    def tell_sibling():
        pl.semaphore_signal(told, inc=1, device_id=(d, sibling), device_id_type=MESH)

    @pl.when(core == 0)
    def _():
        pl.semaphore_wait(barrier, 2 * early_peers + half_cols - 1 + 1 + back)
        tell_sibling()

    @pl.when(core == 1)
    def _():
        pl.semaphore_wait(told, 1)

    def own_slot(side):
        return xall.at[pl.ds(pl.multiple_of(side * whole + place * seg, seg), seg)]

    def send_far(j, _):
        k = j + 1
        pltpu.make_async_remote_copy(
            src_ref=own_slot(0), dst_ref=own_slot(1), send_sem=insend_sem, recv_sem=far_sem,
            device_id=(lax.rem(d + k, groups), k), device_id_type=MESH,
        ).start()
        return 0

    def send_near(j, _):
        pltpu.make_async_remote_copy(
            src_ref=own_slot(0), dst_ref=own_slot(0), send_sem=insend_sem, recv_sem=near_sem,
            device_id=(d, 2 * peer_chip(j) + core), device_id_type=MESH,
        ).start()
        return 0

    lax.fori_loop(0, half_cols - 1, send_far, 0)
    lax.fori_loop(0, early_peers, send_near, 0)

    @pl.when(core == 1)
    def _():
        pl.semaphore_wait(barrier, 2 * (chips - 1 - early_peers) + half_cols + 1 + back)
        tell_sibling()

    @pl.when(core == 0)
    def _():
        pl.semaphore_wait(told, 1)

    lax.fori_loop(half_cols - 1, cols - 1, send_far, 0)
    lax.fori_loop(early_peers, chips - 1, send_near, 0)

    for load in id_loads:
        load.wait()
    tile_load.wait()

    def flip(q, _):
        for u in range(8):
            flipped[q * 8 + u] = tiles[q * 8 + u].T
        return 0

    lax.fori_loop(0, tiles_n // 8, flip, 0)

    g_id = lax.broadcasted_iota(jnp.int32, (group_blocks, 2 * tiles_n), 0)
    at = lax.rem(g_id, cols)
    col_block = at * seg_blocks + g_id // cols
    h_id = lax.broadcasted_iota(jnp.int32, (group_blocks // 2, 2 * tiles_n), 0)
    half_block = lax.rem(h_id, chips) * 2 * seg_blocks + h_id // chips

    def apply(ids_s, matrices):
        for t in range(tiles_n):
            picked = xf[ids_s[0, t]].astype(jnp.bfloat16)
            terms[t * VECS:(t + 1) * VECS, :] = jnp.dot(
                picked, matrices[t], preferred_element_type=jnp.float32
            )

    def scatter(ids_v, block_of, count, part):
        ids = ids_v[...]
        ids = jnp.concatenate([ids, ids], axis=1)
        select = jnp.where(block_of == ids, 1.0, 0.0).astype(jnp.bfloat16)
        for v in range(VECS):
            t = terms[pl.ds(v, tiles_n, stride=VECS), :]
            hi = t.astype(jnp.bfloat16)
            lo = (t - hi.astype(jnp.float32)).astype(jnp.bfloat16)
            both = jnp.concatenate([hi, lo], axis=0)
            r = jnp.dot(select, both, preferred_element_type=jnp.float32)
            for b in range(seg_blocks):
                part[pl.ds(b * VECS + v, count, stride=seg), :] = r[b * count:(b + 1) * count, :]

    def encode(part, first, count, words):
        for s in range(count):
            p = part[pl.ds(pl.multiple_of(first * seg, seg) + s * seg, seg), :]
            top = jnp.max(jnp.abs(p), axis=0, keepdims=True)
            level = jnp.ceil(jnp.log2(jnp.maximum(top, SMALLEST)) * STEPS)
            scale = jnp.exp2(level * (-1.0 / STEPS)) * FULL
            q = jnp.round(p * scale).astype(jnp.int32)
            words[s, 0:half, :] = (q[:half, :] << 16) | (q[half:, :] & 0xFFFF)
            words[s, half:half + 1, :] = level.astype(jnp.int32)

    def wait_bytes(ref, sem):
        pltpu.make_async_copy(ref, ref, sem).wait()

    def load_inputs(first):
        for e in range(cols):
            part = xall[pl.ds(pl.multiple_of(first, whole) + place_of(e) * seg, seg), :]
            xf[e * seg_blocks:(e + 1) * seg_blocks] = part.astype(jnp.float32).reshape(
                seg_blocks, VECS, TILE
            )

    wait_bytes(xall.at[pl.ds(0, (chips - 1) * seg)], near_sem)
    same_core = xall.at[pl.ds(pl.multiple_of(core * chips * seg, chips * seg), chips * seg)]
    pltpu.make_async_remote_copy(
        src_ref=same_core, dst_ref=same_core, send_sem=insend_sem, recv_sem=sib_sem,
        device_id=(d, sibling), device_id_type=MESH,
    ).start()
    wait_bytes(xall.at[pl.ds(0, chips * seg)], sib_sem)

    load_inputs(0)
    apply(rows_s, tiles)
    scatter(cols_v, col_block, cols, pcol)
    encode(pcol, 0, cols, col_words)

    def send_col(k, _):
        pltpu.make_async_remote_copy(
            src_ref=col_words.at[k], dst_ref=got.at[chips + c],
            send_sem=outsend_sem, recv_sem=col_sem,
            device_id=(far_d, k), device_id_type=MESH,
        ).start()
        return 0

    @pl.when(c != 0)
    def _():
        lax.fori_loop(0, COL_FIRST, send_col, 0)

    @pl.when(c != 0)
    def _():
        wait_bytes(xall.at[pl.ds(whole, whole)], far_sem)

    load_inputs(whole * ((c + cols - 1) // cols))
    apply(cols_s, flipped)
    scatter(rows_v, half_block + (1 - core) * seg_blocks, chips, theirs)

    @pl.when(c == 0)
    def _():
        for e in range(1, cols, 2):
            theirs[e // 2 * seg:(e // 2 + 1) * seg, :] += pcol[e * seg:(e + 1) * seg, :]

    pltpu.make_async_remote_copy(
        src_ref=theirs, dst_ref=pair, send_sem=pair_sent_sem, recv_sem=pair_sem,
        device_id=(d, sibling), device_id_type=MESH,
    ).start()
    scatter(rows_v, half_block + core * seg_blocks, chips, ours)

    @pl.when(c == 0)
    def _():
        for e in range(0, cols, 2):
            ours[e // 2 * seg:(e // 2 + 1) * seg, :] += pcol[e * seg:(e + 1) * seg, :]

    wait_bytes(pair, pair_sem)
    ours[...] += pair[...]
    encode(ours, 0, chips, row_words)

    def send_row(j, _):
        to = peer_chip(j)
        pltpu.make_async_remote_copy(
            src_ref=row_words.at[to], dst_ref=got.at[chip],
            send_sem=outsend_sem, recv_sem=row_sem,
            device_id=(d, 2 * to + core), device_id_type=MESH,
        ).start()
        return 0

    lax.fori_loop(0, chips - 1, send_row, 0)

    @pl.when((late == 0) & (c != 0))
    def _():
        lax.fori_loop(COL_FIRST, cols, send_col, 0)

    mine = ours[pl.ds(pl.multiple_of(chip * seg, seg), seg), :]
    upper, lower = mine[:half, :], mine[half:, :]

    def add(slot, upper, lower):
        w = got[slot, 0:half, :]
        unit = jnp.exp2(got[slot, half:half + 1, :].astype(jnp.float32) * (1.0 / STEPS)) * (1.0 / FULL)
        upper += (w >> 16).astype(jnp.float32) * unit
        lower += ((w << 16) >> 16).astype(jnp.float32) * unit
        return upper, lower

    wait_bytes(got.at[pl.ds(0, chips - 1)], row_sem)
    for j in range(chips - 1):
        upper, lower = add(peer_chip(j), upper, lower)
    @pl.when(late == 1)
    def _():
        lax.fori_loop(COL_FIRST, cols, send_col, 0)

    wait_bytes(got.at[pl.ds(0, cols - 1)], col_sem)
    for k in range(1, cols):
        upper, lower = add(chips + k, upper, lower)

    total = jnp.concatenate([upper, lower], axis=0)
    for b in range(seg_blocks):
        out_ref[:, b * TILE:(b + 1) * TILE] = total[b * VECS:(b + 1) * VECS, :]

    wait_bytes(xall.at[pl.ds(0, (2 * chips - 1 + cols - 1) * seg)], insend_sem)
    wait_bytes(pair, pair_sent_sem)
    wait_bytes(row_words.at[pl.ds(0, chips - 1)], outsend_sem)

    @pl.when(c != 0)
    def _():
        wait_bytes(col_words, outsend_sem)


def body(block_vectors, tile_blocks, tile_rows, tile_cols):
    vectors, segment = block_vectors.shape
    groups = lax.axis_size("diag")
    cols = lax.axis_size("col")
    tiles_n = tile_blocks.shape[2]
    group_blocks = segment * cols // TILE
    whole = group_blocks * vectors
    seg = whole // cols
    hbm = pl.BlockSpec(memory_space=pltpu.HBM)
    dma = pltpu.SemaphoreType.DMA
    return pl.pallas_call(
        functools.partial(kernel, groups, cols, tiles_n, group_blocks),
        out_shape=jax.ShapeDtypeStruct((vectors, segment), jnp.float32),
        in_specs=[hbm, hbm, hbm, hbm],
        out_specs=pl.BlockSpec(memory_space=pltpu.VMEM),
        scratch_shapes=[
            pltpu.VMEM((vectors, segment), jnp.bfloat16),
            pltpu.SMEM((1, tiles_n), jnp.int32),
            pltpu.SMEM((1, tiles_n), jnp.int32),
            pltpu.VMEM((1, tiles_n), jnp.int32),
            pltpu.VMEM((1, tiles_n), jnp.int32),
            pltpu.VMEM((tiles_n, TILE, TILE), jnp.bfloat16),
            pltpu.VMEM((tiles_n, TILE, TILE), jnp.bfloat16),
            pltpu.VMEM((2 * whole, TILE), jnp.bfloat16),
            pltpu.VMEM((group_blocks, vectors, TILE), jnp.float32),
            pltpu.VMEM((tiles_n * vectors, TILE), jnp.float32),
            pltpu.VMEM((whole // 2, TILE), jnp.float32),
            pltpu.VMEM((whole // 2, TILE), jnp.float32),
            pltpu.VMEM((whole, TILE), jnp.float32),
            pltpu.VMEM((whole // 2, TILE), jnp.float32),
            pltpu.VMEM((cols // 2, seg // 2 + 1, TILE), jnp.int32),
            pltpu.VMEM((cols, seg // 2 + 1, TILE), jnp.int32),
            pltpu.VMEM((cols // 2 + cols, seg // 2 + 1, TILE), jnp.int32),
            dma, dma((4,)), dma, dma, dma, dma, dma, dma, dma, dma, dma, dma,
            pltpu.SemaphoreType.REGULAR,
        ],
        compiler_params=pltpu.CompilerParams(
            collective_id=0, has_side_effects=True, vmem_limit_bytes=32 * 1024 * 1024
        ),
    )(*[pltpu.with_memory_space_constraint(a, pltpu.HBM) for a in (block_vectors, tile_rows, tile_cols, tile_blocks)])


def solution(mesh):
    return jax.shard_map(
        body,
        mesh=mesh,
        in_specs=(
            P(None, ("diag", "col")),
            P("diag", "col", None, None, None),
            P("diag", "col", None),
            P("diag", "col", None),
        ),
        out_specs=P(None, ("diag", "col")),
        check_vma=False,
    )
```

```python
import functools

import jax
import jax.numpy as jnp
from jax import lax
from jax.experimental import pallas as pl
from jax.experimental.pallas import tpu as pltpu
from jax.sharding import PartitionSpec as P

MESH = pl.DeviceIdType.MESH
TILE = 128
VECS = 8
STEPS = 64.0
FULL = 32700.0
SMALLEST = 2.0 ** -110
COL_FIRST = 8


def kernel(
    groups, cols, tiles_n, group_blocks,
    x_hbm, rows_hbm, cols_hbm, tiles_hbm, out_ref,
    x_own, rows_s, cols_s, rows_v, cols_v, tiles, flipped, xall, xf, terms, ours, theirs, pcol, pair,
    row_words, col_words, got,
    x_sem, ids_sem, tile_sem, near_sem, sib_sem, far_sem, pair_sem, pair_sent_sem, row_sem, col_sem,
    insend_sem, outsend_sem, told,
):
    seg_blocks = group_blocks // cols
    seg = seg_blocks * VECS
    half = seg // 2
    whole = group_blocks * VECS
    d = lax.axis_index("diag")
    c = lax.axis_index("col")
    far_d = lax.rem(d - c + groups, groups)

    x_load = pltpu.make_async_copy(x_hbm, x_own, x_sem)
    x_load.start()
    id_loads = [
        pltpu.make_async_copy(src.at[0], dst, ids_sem.at[n])
        for n, (src, dst) in enumerate(
            ((rows_hbm, rows_s), (cols_hbm, cols_s), (rows_hbm, rows_v), (cols_hbm, cols_v))
        )
    ]
    for load in id_loads:
        load.start()
    tile_load = pltpu.make_async_copy(tiles_hbm.at[0, 0], tiles, tile_sem)
    tile_load.start()

    chips = cols // 2
    chip = c // 2
    core = lax.rem(c, 2)
    sibling = 2 * chip + 1 - core
    place = core * chips + chip

    def place_of(e):
        return (e % 2) * chips + e // 2

    def peer_chip(j):
        return j + (j + chips - chip) // chips

    half_chips = chips // 2
    half_cols = cols // 2
    late = chip // half_chips
    early_peers = half_chips - 1 + late
    barrier = pltpu.get_barrier_semaphore()

    def greet_far(q, _):
        pl.semaphore_signal(barrier, inc=1, device_id=(far_d, 2 * q + late), device_id_type=MESH)
        return 0

    def greet_group(j, _):
        pl.semaphore_signal(
            barrier, inc=1, device_id=(d, 2 * peer_chip(j) + late), device_id_type=MESH
        )
        return 0

    @pl.when(c != 0)
    def _():
        lax.fori_loop(0, chips, greet_far, 0)

    lax.fori_loop(0, chips - 1, greet_group, 0)
    pl.semaphore_signal(barrier, inc=1, device_id=(d, sibling), device_id_type=MESH)

    def greet_back(k, _):
        pl.semaphore_signal(
            barrier, inc=1, device_id=(lax.rem(d + k, groups), 2 * (k // 2) + late),
            device_id_type=MESH,
        )
        return 0

    lax.fori_loop(1, cols, greet_back, 0)
    back = half_cols * (1 + (chip + chips - 1) // chips)

    x_load.wait()
    x = x_own[...]
    own = jnp.concatenate([x[:, b * TILE:(b + 1) * TILE] for b in range(seg_blocks)], axis=0)
    xall[pl.ds(pl.multiple_of(place * seg, seg), seg), :] = own

    def tell_sibling():
        pl.semaphore_signal(told, inc=1, device_id=(d, sibling), device_id_type=MESH)

    @pl.when(core == 0)
    def _():
        pl.semaphore_wait(barrier, 2 * early_peers + half_cols - 1 + 1 + back)
        tell_sibling()

    @pl.when(core == 1)
    def _():
        pl.semaphore_wait(told, 1)

    def own_slot(side):
        return xall.at[pl.ds(pl.multiple_of(side * whole + place * seg, seg), seg)]

    def send_far(j, _):
        k = j + 1
        pltpu.make_async_remote_copy(
            src_ref=own_slot(0), dst_ref=own_slot(1), send_sem=insend_sem, recv_sem=far_sem,
            device_id=(lax.rem(d + k, groups), k), device_id_type=MESH,
        ).start()
        return 0

    def send_near(j, _):
        pltpu.make_async_remote_copy(
            src_ref=own_slot(0), dst_ref=own_slot(0), send_sem=insend_sem, recv_sem=near_sem,
            device_id=(d, 2 * peer_chip(j) + core), device_id_type=MESH,
        ).start()
        return 0

    lax.fori_loop(0, half_cols - 1, send_far, 0)
    lax.fori_loop(0, early_peers, send_near, 0)

    @pl.when(core == 1)
    def _():
        pl.semaphore_wait(barrier, 2 * (chips - 1 - early_peers) + half_cols + 1 + back)
        tell_sibling()

    @pl.when(core == 0)
    def _():
        pl.semaphore_wait(told, 1)

    lax.fori_loop(half_cols - 1, cols - 1, send_far, 0)
    lax.fori_loop(early_peers, chips - 1, send_near, 0)

    for load in id_loads:
        load.wait()
    tile_load.wait()

    def flip(q, _):
        for u in range(8):
            flipped[q * 8 + u] = tiles[q * 8 + u].T
        return 0

    lax.fori_loop(0, tiles_n // 8, flip, 0)

    g_id = lax.broadcasted_iota(jnp.int32, (group_blocks, 2 * tiles_n), 0)
    at = lax.rem(g_id, cols)
    col_block = at * seg_blocks + g_id // cols
    h_id = lax.broadcasted_iota(jnp.int32, (group_blocks // 2, 2 * tiles_n), 0)
    half_block = lax.rem(h_id, chips) * 2 * seg_blocks + h_id // chips

    def apply(ids_s, matrices):
        for t in range(tiles_n):
            picked = xf[ids_s[0, t]].astype(jnp.bfloat16)
            terms[t * VECS:(t + 1) * VECS, :] = jnp.dot(
                picked, matrices[t], preferred_element_type=jnp.float32
            )

    def scatter(ids_v, block_of, count, part):
        ids = ids_v[...]
        ids = jnp.concatenate([ids, ids], axis=1)
        select = jnp.where(block_of == ids, 1.0, 0.0).astype(jnp.bfloat16)
        for v in range(VECS):
            t = terms[pl.ds(v, tiles_n, stride=VECS), :]
            hi = t.astype(jnp.bfloat16)
            lo = (t - hi.astype(jnp.float32)).astype(jnp.bfloat16)
            both = jnp.concatenate([hi, lo], axis=0)
            r = jnp.dot(select, both, preferred_element_type=jnp.float32)
            for b in range(seg_blocks):
                part[pl.ds(b * VECS + v, count, stride=seg), :] = r[b * count:(b + 1) * count, :]

    def encode(part, first, count, words):
        for s in range(count):
            p = part[pl.ds(pl.multiple_of(first * seg, seg) + s * seg, seg), :]
            top = jnp.max(jnp.abs(p), axis=0, keepdims=True)
            level = jnp.ceil(jnp.log2(jnp.maximum(top, SMALLEST)) * STEPS)
            scale = jnp.exp2(level * (-1.0 / STEPS)) * FULL
            q = jnp.round(p * scale).astype(jnp.int32)
            words[s, 0:half, :] = (q[:half, :] << 16) | (q[half:, :] & 0xFFFF)
            words[s, half:half + 1, :] = level.astype(jnp.int32)

    def wait_bytes(ref, sem):
        pltpu.make_async_copy(ref, ref, sem).wait()

    def load_inputs(first):
        for e in range(cols):
            part = xall[pl.ds(pl.multiple_of(first, whole) + place_of(e) * seg, seg), :]
            xf[e * seg_blocks:(e + 1) * seg_blocks] = part.astype(jnp.float32).reshape(
                seg_blocks, VECS, TILE
            )

    wait_bytes(xall.at[pl.ds(0, (chips - 1) * seg)], near_sem)
    same_core = xall.at[pl.ds(pl.multiple_of(core * chips * seg, chips * seg), chips * seg)]
    pltpu.make_async_remote_copy(
        src_ref=same_core, dst_ref=same_core, send_sem=insend_sem, recv_sem=sib_sem,
        device_id=(d, sibling), device_id_type=MESH,
    ).start()
    wait_bytes(xall.at[pl.ds(0, chips * seg)], sib_sem)

    load_inputs(0)
    apply(rows_s, tiles)
    scatter(cols_v, col_block, cols, pcol)
    encode(pcol, 0, cols, col_words)

    def send_col(k, _):
        pltpu.make_async_remote_copy(
            src_ref=col_words.at[k], dst_ref=got.at[chips + c],
            send_sem=outsend_sem, recv_sem=col_sem.at[late],
            device_id=(far_d, k), device_id_type=MESH,
        ).start()
        return 0

    @pl.when(c != 0)
    def _():
        lax.fori_loop(0, COL_FIRST, send_col, 0)

    @pl.when(c != 0)
    def _():
        wait_bytes(xall.at[pl.ds(whole, whole)], far_sem)

    load_inputs(whole * ((c + cols - 1) // cols))
    apply(cols_s, flipped)
    scatter(rows_v, half_block + (1 - core) * seg_blocks, chips, theirs)

    @pl.when(c == 0)
    def _():
        for e in range(1, cols, 2):
            theirs[e // 2 * seg:(e // 2 + 1) * seg, :] += pcol[e * seg:(e + 1) * seg, :]

    pltpu.make_async_remote_copy(
        src_ref=theirs, dst_ref=pair, send_sem=pair_sent_sem, recv_sem=pair_sem,
        device_id=(d, sibling), device_id_type=MESH,
    ).start()
    scatter(rows_v, half_block + core * seg_blocks, chips, ours)

    @pl.when(c == 0)
    def _():
        for e in range(0, cols, 2):
            ours[e // 2 * seg:(e // 2 + 1) * seg, :] += pcol[e * seg:(e + 1) * seg, :]

    wait_bytes(pair, pair_sem)
    ours[...] += pair[...]
    encode(ours, 0, chips, row_words)

    def send_row(j, _):
        to = peer_chip(j)
        pltpu.make_async_remote_copy(
            src_ref=row_words.at[to], dst_ref=got.at[chip],
            send_sem=outsend_sem, recv_sem=row_sem,
            device_id=(d, 2 * to + core), device_id_type=MESH,
        ).start()
        return 0

    lax.fori_loop(0, chips - 1, send_row, 0)

    @pl.when((late == 0) & (c != 0))
    def _():
        lax.fori_loop(COL_FIRST, cols, send_col, 0)

    mine = ours[pl.ds(pl.multiple_of(chip * seg, seg), seg), :]
    upper, lower = mine[:half, :], mine[half:, :]

    def add(slot, upper, lower):
        w = got[slot, 0:half, :]
        unit = jnp.exp2(got[slot, half:half + 1, :].astype(jnp.float32) * (1.0 / STEPS)) * (1.0 / FULL)
        upper += (w >> 16).astype(jnp.float32) * unit
        lower += ((w << 16) >> 16).astype(jnp.float32) * unit
        return upper, lower

    wait_bytes(got.at[pl.ds(0, half_cols - 1)], col_sem.at[0])
    for k in range(1, half_cols):
        upper, lower = add(chips + k, upper, lower)
    wait_bytes(got.at[pl.ds(0, chips - 1)], row_sem)
    for j in range(chips - 1):
        upper, lower = add(peer_chip(j), upper, lower)
    @pl.when(late == 1)
    def _():
        lax.fori_loop(COL_FIRST, cols, send_col, 0)

    wait_bytes(got.at[pl.ds(0, half_cols)], col_sem.at[1])
    for k in range(half_cols, cols):
        upper, lower = add(chips + k, upper, lower)

    total = jnp.concatenate([upper, lower], axis=0)
    for b in range(seg_blocks):
        out_ref[:, b * TILE:(b + 1) * TILE] = total[b * VECS:(b + 1) * VECS, :]

    wait_bytes(xall.at[pl.ds(0, (2 * chips - 1 + cols - 1) * seg)], insend_sem)
    wait_bytes(pair, pair_sent_sem)
    wait_bytes(row_words.at[pl.ds(0, chips - 1)], outsend_sem)

    @pl.when(c != 0)
    def _():
        wait_bytes(col_words, outsend_sem)


def body(block_vectors, tile_blocks, tile_rows, tile_cols):
    vectors, segment = block_vectors.shape
    groups = lax.axis_size("diag")
    cols = lax.axis_size("col")
    tiles_n = tile_blocks.shape[2]
    group_blocks = segment * cols // TILE
    whole = group_blocks * vectors
    seg = whole // cols
    hbm = pl.BlockSpec(memory_space=pltpu.HBM)
    dma = pltpu.SemaphoreType.DMA
    return pl.pallas_call(
        functools.partial(kernel, groups, cols, tiles_n, group_blocks),
        out_shape=jax.ShapeDtypeStruct((vectors, segment), jnp.float32),
        in_specs=[hbm, hbm, hbm, hbm],
        out_specs=pl.BlockSpec(memory_space=pltpu.VMEM),
        scratch_shapes=[
            pltpu.VMEM((vectors, segment), jnp.bfloat16),
            pltpu.SMEM((1, tiles_n), jnp.int32),
            pltpu.SMEM((1, tiles_n), jnp.int32),
            pltpu.VMEM((1, tiles_n), jnp.int32),
            pltpu.VMEM((1, tiles_n), jnp.int32),
            pltpu.VMEM((tiles_n, TILE, TILE), jnp.bfloat16),
            pltpu.VMEM((tiles_n, TILE, TILE), jnp.bfloat16),
            pltpu.VMEM((2 * whole, TILE), jnp.bfloat16),
            pltpu.VMEM((group_blocks, vectors, TILE), jnp.float32),
            pltpu.VMEM((tiles_n * vectors, TILE), jnp.float32),
            pltpu.VMEM((whole // 2, TILE), jnp.float32),
            pltpu.VMEM((whole // 2, TILE), jnp.float32),
            pltpu.VMEM((whole, TILE), jnp.float32),
            pltpu.VMEM((whole // 2, TILE), jnp.float32),
            pltpu.VMEM((cols // 2, seg // 2 + 1, TILE), jnp.int32),
            pltpu.VMEM((cols, seg // 2 + 1, TILE), jnp.int32),
            pltpu.VMEM((cols // 2 + cols, seg // 2 + 1, TILE), jnp.int32),
            dma, dma((4,)), dma, dma, dma, dma, dma, dma, dma, dma((2,)), dma, dma,
            pltpu.SemaphoreType.REGULAR,
        ],
        compiler_params=pltpu.CompilerParams(
            collective_id=0, has_side_effects=True, vmem_limit_bytes=32 * 1024 * 1024
        ),
    )(*[pltpu.with_memory_space_constraint(a, pltpu.HBM) for a in (block_vectors, tile_rows, tile_cols, tile_blocks)])


def solution(mesh):
    return jax.shard_map(
        body,
        mesh=mesh,
        in_specs=(
            P(None, ("diag", "col")),
            P("diag", "col", None, None, None),
            P("diag", "col", None),
            P("diag", "col", None),
        ),
        out_specs=P(None, ("diag", "col")),
        check_vma=False,
    )
```
